32 devices in a mesh: groups: 2 (over x), sub: 16 (over z, y, core).
Axes of the slice: x: 2, y: 2, z: 4, core: 2. Of those that a mesh axis runs over, the one named last changes fastest.
Arguments:
- source_field: float32 [128, 32768], P('groups', 'sub'), parts along dimension 0, may hold values from -6 to 6
- inject_amp: float32 [128], P('groups'), parts along dimension 0, may hold values from 1 to 4
- inject_nodes: int32 [2, 128], P(None, 'groups'), parts along dimension 1, may hold values from 0 to 32767
- node_diag: float32 [32768], P('sub'), may hold values from 3 to 12
- blocks: float32 [256, 7, 128, 128], P('sub'), may hold values from -0.1875 to 0.1875
- pattern: int32 [256, 7], P('sub'), may hold values from 0 to 15
- local_inv: float32 [256, 128, 128], P('sub')
- iface_nodes: int32 [16, 4, 256], P('sub'), may hold values from 0 to 2047
- iface_count: int32 [16, 4], P('sub'), may hold values from 0 to 256, as said below
- iface_wt: float32 [16, 4, 256], P('sub'), may hold values from 0.5 to 2
- aggregate: int32 [32768], P('sub'), may hold values from 0 to 7
- coarse_inv: float32 [128, 128], P('sub')
Outputs:
- solution: float32 [128, 32768], P('groups', 'sub'), parts along dimension 0
- residual: float32 [128, 32768], P('groups', 'sub'), parts along dimension 0
The draws below stay inside these ranges and needn't reach their ends.
There are 2 independent parts, one for each index of `groups`. The reference program is written for one: setup_inputs(seed, part) draws one part's arguments, and reference() takes and returns one part's arrays. A program takes and returns all parts, laid end to end along the dimension named above; an argument that names none is the same for every part. Nothing has to cross between parts.
Inputs may be any that keep to these rules, and one draw needn't show every extreme that they name: `iface_count`: for the two subdomains of a pair the counts of their facing slots are equal; counts toward subdomains outside the mesh are 0; some pair uses all 256 slots.
All inputs are finite; a program needn't handle non-finite values.
Results may differ from the reference program's by a relative error of at most 0.00012.
Values sent between devices are 32-bit elements; how exact they have to be, the bound alone decides.
A program may use at most 64 MiB of HBM per device.

```python
import math
import jax
import jax.numpy as jnp
from jax import lax

COLS = 64
BS = 128
NBLK = 16
KB = 7
IFMAX = 256
AGG_DEV = 8
ITERS = 3
NODE_DEV = 2048
NODES = 32768
BLOCKS = 256
NC = 128
N_SUB = 16


def draw_local_inv(key, part):
    key = jax.random.fold_in(key, 5)
    first, second = jax.random.split(key)
    diagonal = 1.0 / jax.random.uniform(first, (BLOCKS, BS), jnp.float32, 3.0, 12.0)
    noise = jax.random.normal(second, (BLOCKS, BS, BS), jnp.float32) * (0.25 / (6.0 * BS ** 0.5))
    return jnp.eye(BS, dtype=jnp.float32)[None, :, :] * diagonal[:, None, :] + noise


def draw_coarse_inv(key, part):
    key = jax.random.fold_in(key, 7)
    noise = jax.random.normal(key, (NC, NC), jnp.float32) * (0.3 / NC ** 0.5)
    factor = 0.5 / (NODE_DEV / AGG_DEV) ** 0.5
    return (jnp.eye(NC, dtype=jnp.float32) + noise) * factor


def draw_iface_count(key, part):
    key = jax.random.fold_in(key, 11)
    paired = jax.random.randint(key, (N_SUB, 2), IFMAX // 4, IFMAX + 1)
    paired = paired.at[0, 0].set(IFMAX)
    device = jnp.arange(N_SUB, dtype=jnp.int32)
    columns = []
    for offset in (-2, -1, 1, 2):
        reach = abs(offset)
        if offset > 0:
            values = paired[:, reach - 1]
            valid = device + reach < N_SUB
        else:
            values = jnp.roll(paired[:, reach - 1], reach)
            valid = device - reach >= 0
        columns.append(jnp.where(valid, values, 0))
    return jnp.stack(columns, axis=1).astype(jnp.int32)


def touch_ends(array, own_key, low, high):
    longest = array.shape.index(max(array.shape))
    spots = []
    for shift in (0, 1):
        where = [jax.random.randint(jax.random.fold_in(own_key, axis), (), 0, length) for axis, length in enumerate(array.shape)]
        where[longest] = (where[longest] + shift) % array.shape[longest]
        spots.append(tuple(where))
    return array.at[spots[0]].set(low).at[spots[1]].set(high)


def level_of(stream_key, dims, cuts, low, largest):
    gain = 1.0
    for dim, blocks in cuts:
        steps = jax.random.uniform(jax.random.fold_in(jax.random.fold_in(stream_key, 6), dim), (blocks,), jnp.float32, low / len(cuts), largest / len(cuts))
        gain = gain * jnp.repeat(jnp.exp(steps), dims[dim] // blocks).reshape((-1,) + (1,) * (len(dims) - 1 - dim))
    return gain


def gaussian(rng, extent, deviation, most, cuts=(), held_as=jnp.bfloat16):
    gain = level_of(rng, extent, cuts, -0.22, 0.18) if cuts else 1.0
    entries = jax.random.normal(rng, extent, jnp.float32) * deviation * gain
    return jnp.minimum(jnp.maximum(entries, -most), most).astype(held_as)


def setup_inputs(seed: int = 0, part: int = 0) -> dict:
    arg_keys = jax.random.split(jax.random.key(seed), 13)
    own_keys = jax.random.split(jax.random.fold_in(arg_keys[12], part), 13)
    source_field = gaussian(own_keys[0], (COLS, NODES), 1.0, 6.0, ((1, 16),), jnp.float32)
    inject_amp = jnp.clip(jnp.exp(jax.random.uniform(own_keys[1], (COLS,), jnp.float32, math.log(1.0), math.log(4.0))), 1.0, 4.0)
    inject_nodes = touch_ends(jax.random.randint(own_keys[2], (2, COLS), 0, NODES), jax.random.fold_in(own_keys[2], 1), 0, NODES - 1).astype(jnp.int32)
    node_diag = jnp.clip(jnp.exp(math.log(12.0) - 1.3862944 * jax.random.uniform(arg_keys[3], (NODES,), jnp.float32) ** level_of(arg_keys[3], (NODES,), ((0, 16),), -0.2, 0.2)), 3.0, 12.0)
    blocks = gaussian(arg_keys[4], (BLOCKS, KB, BS, BS), (BS * KB) ** -0.5, 0.1875, ((0, 16),), jnp.float32)
    pattern = touch_ends(jax.random.randint(arg_keys[5], (BLOCKS, KB), 0, NBLK), jax.random.fold_in(arg_keys[5], 1), 0, NBLK - 1).astype(jnp.int32)
    local_inv = draw_local_inv(jax.random.fold_in(arg_keys[12], 71), part)
    iface_nodes = touch_ends(jax.random.randint(arg_keys[7], (N_SUB, 4, IFMAX), 0, NODE_DEV), jax.random.fold_in(arg_keys[7], 1), 0, NODE_DEV - 1).astype(jnp.int32)
    iface_count = draw_iface_count(jax.random.fold_in(arg_keys[12], 71), part)
    iface_wt = jnp.clip(0.5 + 1.5 * jax.random.uniform(arg_keys[9], (N_SUB, 4, IFMAX), jnp.float32) ** level_of(arg_keys[9], (N_SUB, 4, IFMAX), ((0, 16),), -0.2, 0.2), 0.5, 2.0)
    aggregate = touch_ends(jax.random.randint(arg_keys[10], (NODES,), 0, AGG_DEV), jax.random.fold_in(arg_keys[10], 1), 0, AGG_DEV - 1).astype(jnp.int32)
    coarse_inv = draw_coarse_inv(jax.random.fold_in(arg_keys[12], 71), part)
    return dict(source_field=source_field, inject_amp=inject_amp, inject_nodes=inject_nodes, node_diag=node_diag, blocks=blocks, pattern=pattern, local_inv=local_inv, iface_nodes=iface_nodes, iface_count=iface_count, iface_wt=iface_wt, aggregate=aggregate, coarse_inv=coarse_inv)


OFFSETS = (-2, -1, 1, 2)
epsilon = 1e-6
HIGH = lax.Precision.HIGHEST


def shift_devices(sent, offset):
    blanks = jnp.zeros((sent.shape[0], abs(offset), sent.shape[2]), jnp.float32)
    if offset > 0:
        return jnp.concatenate([sent[:, offset:], blanks], axis=1)
    return jnp.concatenate([blanks, sent[:, :offset]], axis=1)


def reference(source_field, inject_amp, inject_nodes, node_diag, blocks, pattern, local_inv, iface_nodes, iface_count, iface_wt, aggregate, coarse_inv):
    global_node = jnp.arange(NODES, dtype=jnp.int32)
    at_source = (inject_nodes[0][:, None] == global_node[None, :]).astype(jnp.float32)
    at_sink = (inject_nodes[1][:, None] == global_node[None, :]).astype(jnp.float32)
    rhs = source_field + inject_amp[:, None] * (at_source - at_sink)
    blocks_all = blocks.reshape(N_SUB, NBLK, KB, BS, BS)
    pattern_all = pattern.reshape(N_SUB, NBLK, KB)
    inverse_all = local_inv.reshape(N_SUB, NBLK, BS, BS)
    membership = (aggregate.reshape(N_SUB, NODE_DEV)[:, :, None] == jnp.arange(AGG_DEV, dtype=jnp.int32)[None, None, :]).astype(jnp.float32)
    slot_live = jnp.arange(IFMAX, dtype=jnp.int32)[None, None, :] < iface_count[:, :, None]
    scaled = iface_wt * slot_live.astype(jnp.float32)

    def apply_local(pieces):
        block_set, block_cols, values = pieces
        picked = values[:, block_cols, :]
        return jnp.einsum('ikab,cikb->cia', block_set, picked, precision=HIGH)

    def operate(field):
        split_field = field.reshape(COLS, N_SUB, NBLK, BS).transpose(1, 0, 2, 3)
        coupled = lax.map(apply_local, (blocks_all, pattern_all, split_field))
        coupled = coupled.transpose(1, 0, 2, 3).reshape(COLS, NODES)
        result = (node_diag[None, :] * field + coupled).reshape(COLS, N_SUB, NODE_DEV)
        field_three = field.reshape(COLS, N_SUB, NODE_DEV)
        for slot_index, offset in enumerate(OFFSETS):
            sent = jnp.take_along_axis(field_three, iface_nodes[None, :, 3 - slot_index, :], axis=2)
            arrived = shift_devices(sent, offset) * scaled[None, :, slot_index, :]
            result = jax.vmap(lambda target, where, amount: target.at[:, where].add(-amount), in_axes=(1, 0, 1), out_axes=1)(result, iface_nodes[:, slot_index, :], arrived)
        return result.reshape(COLS, NODES)

    solution = jnp.zeros((COLS, NODES), jnp.float32)
    residual = rhs
    for sweep in range(ITERS):
        resid_three = residual.reshape(COLS, N_SUB, NODE_DEV)
        coarse = jnp.einsum('csn,sna->csa', resid_three, membership, precision=HIGH).reshape(COLS, NC)
        coarse_sol = jnp.dot(coarse, coarse_inv.T, precision=HIGH).reshape(COLS, N_SUB, AGG_DEV)
        prolonged = jnp.einsum('csa,sna->csn', coarse_sol, membership, precision=HIGH).reshape(COLS, NODES)
        local_part = jnp.einsum('sjab,csjb->csja', inverse_all, residual.reshape(COLS, N_SUB, NBLK, BS), precision=HIGH).reshape(COLS, NODES)
        update = local_part + prolonged
        image_vec = operate(update)
        step_len = jnp.sum(residual * image_vec, axis=1) / (jnp.sum(image_vec * image_vec, axis=1) + epsilon)
        solution = solution + step_len[:, None] * update
        residual = residual - step_len[:, None] * image_vec
    return solution, residual
```

```python
import functools
import jax
import jax.numpy as jnp
from jax import lax
from jax.experimental import pallas as pl
from jax.experimental.pallas import tpu as pltpu
from jax.sharding import PartitionSpec as P

ITERS = 3
OFFSETS = (-2, -1, 1, 2)
EPSILON = 1e-06
HIGH = lax.Precision.HIGHEST
F32 = jnp.float32
BF16 = jnp.bfloat16
NT = (((1,), (1,)), ((), ()))


def split(value):
    high = value.astype(BF16)
    low = (value - high.astype(F32)).astype(BF16)
    return jnp.concatenate([high, low], axis=0)


def nt_dot(left, right):
    return lax.dot_general(left, right, NT, preferred_element_type=F32)


def fold(product, columns, width):
    return (
        product[:columns, :width]
        + product[:columns, width:]
        + product[columns : 2 * columns, :width]
    )


def kernel(
    source_ref,
    amp_ref,
    inject_ref,
    diag_ref,
    blocks_hbm,
    pattern_ref,
    inverse_hbm,
    nodes_ref,
    count_ref,
    weight_ref,
    aggregate_ref,
    coarse_ref,
    x_ref,
    r_ref,
    raw,
    raw_inv,
    mat,
    inv,
    onehot,
    split_v,
    split_l,
    member,
    extra,
    local,
    upd,
    img,
    out_y,
    ap,
    scaled,
    tile,
    near_inv,
    sums,
    outbox,
    inbox,
    raw_sem,
    inv_sem,
    sum_send,
    sum_recv,
    face_send,
    face_recv,
    near_send,
    near_recv,
):
    n_sub = lax.axis_size("sub")
    me = lax.axis_index("sub")
    columns, node_count = source_ref.shape
    rows, kept, size, _ = blocks_hbm.shape
    agg = coarse_ref.shape[0]
    slots = nodes_ref.shape[2]
    double = 2 * columns
    near = [me + offset for offset in OFFSETS]
    there = [jnp.logical_and(other >= 0, other < n_sub) for other in near]

    barrier = pltpu.get_barrier_semaphore()

    def greet(step, carry):
        other = lax.rem(me + step, n_sub)
        pl.semaphore_signal(
            barrier, inc=1, device_id={"sub": other}, device_id_type=pl.DeviceIdType.MESH
        )
        return carry

    def inverse_copy():
        return pltpu.make_async_copy(inverse_hbm, raw_inv, inv_sem)

    def block_copy(i):
        return pltpu.make_async_copy(blocks_hbm.at[i], raw.at[i], raw_sem.at[i])

    inverse_copy().start()
    for i in range(rows):
        block_copy(i).start()

    inbox[...] = jnp.zeros_like(inbox)
    near_inv[...] = jnp.zeros_like(near_inv)
    near_inv[0:agg, :] = coarse_ref[...]
    lax.fori_loop(1, n_sub, greet, 0)

    tile[...] = jnp.zeros_like(tile)
    tile[0:2, 0:columns] = inject_ref[...].astype(F32)
    tile[2:3, 0:columns] = amp_ref[...]
    turned = tile[...].T
    first_node = me * node_count
    at_source = turned[:columns, 0:1].astype(jnp.int32) - first_node
    at_sink = turned[:columns, 1:2].astype(jnp.int32) - first_node
    amp = turned[:columns, 2:3]
    lane = lax.broadcasted_iota(jnp.int32, (columns, size), 1)
    agg_id = lax.broadcasted_iota(jnp.int32, (2 * agg, size), 0)
    for i in range(rows):
        place = slice(i * size, (i + 1) * size)
        node = lane + i * size
        hits = (node == at_source).astype(F32) - (node == at_sink).astype(F32)
        rhs = source_ref[:, place] + amp * hits
        out_y[i] = rhs
        split_v[:, place] = split(rhs)
        belongs = (agg_id == aggregate_ref[:, place]).astype(F32).astype(BF16)
        member[:, place] = belongs
        split_l[i, double : double + 2 * agg, :] = belongs

    pl.semaphore_wait(barrier, n_sub - 1)

    def sum_copy(stage, other):
        return pltpu.make_async_remote_copy(
            src_ref=sums.at[stage, me],
            dst_ref=sums.at[stage, me],
            send_sem=sum_send.at[stage],
            recv_sem=sum_recv.at[stage],
            device_id={"sub": other},
            device_id_type=pl.DeviceIdType.MESH,
        )

    def send_sums(stage):
        def one(step, carry):
            sum_copy(stage, lax.rem(me + step, n_sub)).start()
            return carry

        lax.fori_loop(1, n_sub, one, 0)

    def all_sums(stage, sem):
        span = sums.at[stage, pl.ds(0, n_sub - 1)]
        return pltpu.make_async_copy(span, span, sem.at[stage])

    def face_copy(stage, j):
        depth = columns + agg if stage == 0 else columns
        return pltpu.make_async_remote_copy(
            src_ref=outbox.at[stage, j, pl.ds(0, depth)],
            dst_ref=inbox.at[stage, 3 - j, pl.ds(0, depth)],
            send_sem=face_send.at[stage, j],
            recv_sem=face_recv.at[stage, 3 - j],
            device_id={"sub": near[j]},
            device_id_type=pl.DeviceIdType.MESH,
        )

    def face_arrival(stage, j):
        depth = columns + agg if stage == 0 else columns
        span = inbox.at[stage, j, pl.ds(0, depth)]
        return pltpu.make_async_copy(span, span, face_recv.at[stage, j])

    def near_copy(j):
        return pltpu.make_async_remote_copy(
            src_ref=coarse_ref,
            dst_ref=near_inv.at[pl.ds((4 - j) * agg, agg)],
            send_sem=near_send.at[j],
            recv_sem=near_recv.at[3 - j],
            device_id={"sub": near[j]},
            device_id_type=pl.DeviceIdType.MESH,
        )

    def near_arrival(j):
        span = near_inv.at[pl.ds((1 + j) * agg, agg)]
        return pltpu.make_async_copy(span, span, near_recv.at[j])

    def put_dots():
        def add(i, carry):
            image = img[i]
            return carry[0] + r_now(i) * image, carry[1] + image * image

        zero = jnp.zeros((columns, size), F32)
        ri, ii = lax.fori_loop(0, rows, add, (zero, zero))
        turned = jnp.concatenate([ri, ii], axis=0).T
        return jnp.sum(turned.reshape(size // 8, 8, double), axis=0)

    def r_now(i):
        return out_r[i]

    def step_of(stage):
        total = jnp.sum(sums[stage, :, 8:16, :], axis=(0, 1), keepdims=False)[None, :]
        both = jnp.broadcast_to(total, (size, double)).T
        return both[:columns] / (both[columns:] + EPSILON)

    out_r, y_now, x_now = upd.at[1], upd.at[2], upd.at[3]
    u_now = upd.at[0]

    def keep_rhs(i, carry):
        out_r[i] = out_y[i]
        return carry

    lax.fori_loop(0, rows, keep_rhs, 0)

    for stage in range(ITERS):
        sums[stage, me, 0:8, :] = nt_dot(member[...], split_v[...])[:agg]
        if stage:
            sums[stage, me, 8:16, :] = put_dots()
        else:
            sums[stage, me, 8:16, :] = jnp.zeros((8, double), F32)
        send_sums(stage)
        if stage == 0:
            for j in range(4):
                pl.when(there[j])(near_copy(j).start)
            for j in range(4):
                live = lax.broadcasted_iota(jnp.int32, (1, slots), 1) < count_ref[0, j]
                scaled[:, j * slots : (j + 1) * slots] = jnp.where(
                    live, weight_ref[0, j : j + 1, :], 0.0
                )
            span = 2 * size

            def build(c, carry):
                ids = lax.broadcasted_iota(jnp.int32, (span, slots), 0) + c * span
                for j in range(4):
                    same = ids == nodes_ref[0, j : j + 1, :]
                    onehot[
                        pl.ds(pl.multiple_of(c * span, span), span),
                        j * slots : (j + 1) * slots,
                    ] = jnp.where(same, 1.0, 0.0).astype(BF16)
                return carry

            lax.fori_loop(0, rows // 2, build, 0)
            inverse_copy().wait()

        def solve(half, carry):
            for part in range(2):
                i = 2 * half + part
                if stage == 0:
                    inv[i] = split(raw_inv[i])
                place = pl.ds(pl.multiple_of(i * size, size), size)
                value = fold(nt_dot(split_v[:, place], inv[i]), columns, size)
                local[i] = value
                split_l[i, 0:double, :] = split(value)
            return carry

        lax.fori_loop(0, rows // 2, solve, 0)

        depth = double + 2 * agg if stage == 0 else double
        left = jnp.concatenate([split_l[i, 0:depth, :] for i in range(rows)], axis=1)
        for j in range(4):
            got = jnp.dot(
                left, onehot[:, j * slots : (j + 1) * slots], preferred_element_type=F32
            )
            outbox[stage, j, 0:columns, :] = got[:columns] + got[columns:double]
            if stage == 0:
                outbox[stage, j, columns : columns + agg, :] = got[double : double + agg]
            pl.when(there[j])(face_copy(stage, j).start)

        def apply(half, carry):
            for part in range(2):
                i = 2 * half + part
                if stage == 0:
                    block_copy(i).wait()
                    for k in range(kept):
                        mat[i, :, k * size : (k + 1) * size] = split(raw[i, k])
                picked = jnp.concatenate(
                    [split_l[pattern_ref[i, k], 0:depth, :] for k in range(kept)], axis=1
                )
                product = nt_dot(picked, mat[i])
                place = pl.ds(pl.multiple_of(i * size, size), size)
                diag = diag_ref[:, place]
                y_now[i] = fold(product, columns, size) + diag * local[i]
                if stage == 0:
                    own = product[double : double + agg]
                    mine = split_l[i, double : double + 2 * agg, :].astype(F32)[:agg]
                    ap[i, 0:agg, :] = own[:, :size] + own[:, size:] + diag * mine
            return carry

        lax.fori_loop(0, rows // 2, apply, 0)

        for j in range(4):
            pl.when(there[j])(face_arrival(stage, j).wait)
        pieces = [
            split(inbox[stage, j, 0:columns, :] * scaled[:, j * slots : (j + 1) * slots])
            for j in range(4)
        ]
        left = jnp.concatenate(pieces, axis=1)
        if stage == 0:
            strips = []
            for j in range(4):
                strip = inbox[stage, j, columns : columns + agg, :]
                strip = strip * scaled[:, j * slots : (j + 1) * slots]
                cells = [jnp.zeros((agg, slots), F32)] * 4
                cells[j] = strip
                strips.append(jnp.concatenate(cells, axis=1))
            left = jnp.concatenate([left, split(jnp.concatenate(strips, axis=0))], axis=0)

        def scatter(c, carry):
            span = 2 * size
            chunk = onehot[pl.ds(pl.multiple_of(c * span, span), span), :]
            product = nt_dot(left, chunk)
            for part in range(2):
                piece = product[:, part * size : (part + 1) * size]
                i = 2 * c + part
                y_now[i] = y_now[i] - (piece[:columns] + piece[columns:double])
                if stage == 0:
                    outer = piece[double : double + 4 * agg] + piece[double + 4 * agg :]
                    ap[i, agg : 5 * agg, :] = -outer
                    high = ap[i].astype(BF16).astype(F32)
                    low = ap[i] - high
                    pad = jnp.zeros((agg, size), F32)
                    tail = jnp.zeros((size - 11 * agg, size), F32)
                    extra[i, :, 0:size] = jnp.concatenate(
                        [high, pad, low, tail], axis=0
                    ).astype(BF16)
                    mine = split_l[i, double : double + 2 * agg, :].astype(F32)[:agg]
                    extra[i, :, size : 2 * size] = jnp.concatenate(
                        [mine, jnp.zeros((size - agg, size), F32)], axis=0
                    ).astype(BF16)
            return carry

        lax.fori_loop(0, rows // 2, scatter, 0)

        all_sums(stage, sum_recv).wait()
        if stage == 0:
            for j in range(4):
                pl.when(there[j])(near_arrival(j).wait)
        gathered = sums[stage, :, 0:8, :].reshape(n_sub * agg, double)
        coarse = jnp.dot(near_inv[...], gathered, precision=HIGH, preferred_element_type=F32)
        turned = jnp.concatenate(
            [coarse, jnp.zeros((agg, double), F32), coarse, jnp.zeros((size - 11 * agg, double), F32)],
            axis=0,
        ).T
        coarse_split = split(turned[:columns] + turned[columns:])
        if stage:
            step = step_of(stage)

        def finish(half, carry):
            for part in range(2):
                i = 2 * half + part
                product = jnp.dot(coarse_split, extra[i], preferred_element_type=F32)
                product = product[:columns] + product[columns:]
                image = y_now[i] + product[:, :size]
                update = local[i] + product[:, size:]
                if stage == 0:
                    new_u, new_w = update, image
                    x_now[i] = jnp.zeros_like(update)
                else:
                    old_u, old_w = u_now[i], img[i]
                    x_now[i] = x_now[i] + step * old_u
                    out_r[i] = out_r[i] - step * old_w
                    new_u, new_w = old_u - step * update, old_w - step * image
                u_now[i] = new_u
                img[i] = new_w
                if stage < ITERS - 1:
                    place = pl.ds(pl.multiple_of(i * size, size), size)
                    split_v[:, place] = split(new_w)
            return carry

        lax.fori_loop(0, rows // 2, finish, 0)

    sums[ITERS, me, 0:8, :] = jnp.zeros((8, double), F32)
    sums[ITERS, me, 8:16, :] = put_dots()
    send_sums(ITERS)
    all_sums(ITERS, sum_recv).wait()
    step = step_of(ITERS)
    for i in range(rows):
        place = slice(i * size, (i + 1) * size)
        x_ref[:, place] = x_now[i] + step * u_now[i]
        r_ref[:, place] = out_r[i] - step * img[i]

    for stage in range(ITERS + 1):
        all_sums(stage, sum_send).wait()
    for j in range(4):
        pl.when(there[j])(near_copy(j).wait_send)
        for stage in range(ITERS):
            pl.when(there[j])(face_copy(stage, j).wait_send)


def shards(
    source_field,
    inject_amp,
    inject_nodes,
    node_diag,
    blocks,
    pattern,
    local_inv,
    iface_nodes,
    iface_count,
    iface_wt,
    aggregate,
    coarse_inv,
):
    columns, node_count = source_field.shape
    rows, kept, size, _ = blocks.shape
    agg, n_coarse = coarse_inv.shape
    slots = iface_wt.shape[2]
    n_sub = lax.axis_size("sub")
    vmem = pl.BlockSpec(memory_space=pltpu.VMEM)
    smem = pl.BlockSpec(memory_space=pltpu.SMEM)
    far = pl.BlockSpec(memory_space=pl.ANY)
    field = jax.ShapeDtypeStruct((columns, node_count), F32)
    dma = pltpu.SemaphoreType.DMA
    return pl.pallas_call(
        kernel,
        out_shape=(field, field),
        in_specs=[vmem, vmem, vmem, vmem, far, smem, far, vmem, smem, vmem, vmem, vmem],
        out_specs=(vmem, vmem),
        scratch_shapes=[
            pltpu.VMEM((rows, kept, size, size), F32),
            pltpu.VMEM((rows, size, size), F32),
            pltpu.VMEM((rows, 2 * size, kept * size), BF16),
            pltpu.VMEM((rows, 2 * size, size), BF16),
            pltpu.VMEM((node_count, 4 * slots), BF16),
            pltpu.VMEM((2 * columns, node_count), BF16),
            pltpu.VMEM((rows, 2 * columns + 2 * agg, size), BF16),
            pltpu.VMEM((2 * agg, node_count), BF16),
            pltpu.VMEM((rows, size, 2 * size), BF16),
            pltpu.VMEM((rows, columns, size), F32),
            pltpu.VMEM((4, rows, columns, size), F32),
            pltpu.VMEM((rows, columns, size), F32),
            pltpu.VMEM((rows, columns, size), F32),
            pltpu.VMEM((rows, 5 * agg, size), F32),
            pltpu.VMEM((1, 4 * slots), F32),
            pltpu.VMEM((size, size), F32),
            pltpu.VMEM((5 * agg, n_coarse), F32),
            pltpu.VMEM((ITERS + 1, n_sub, 16, 2 * columns), F32),
            pltpu.VMEM((ITERS, 4, columns + agg, slots), F32),
            pltpu.VMEM((ITERS, 4, columns + agg, slots), F32),
            dma((rows,)),
            dma,
            dma((ITERS + 1,)),
            dma((ITERS + 1,)),
            dma((ITERS, 4)),
            dma((ITERS, 4)),
            dma((4,)),
            dma((4,)),
        ],
        compiler_params=pltpu.CompilerParams(
            collective_id=0, has_side_effects=True, vmem_limit_bytes=56 * 1024 * 1024
        ),
        cost_estimate=pl.CostEstimate(
            flops=4_000_000_000, bytes_accessed=12_000_000, transcendentals=0
        ),
    )(
        source_field,
        inject_amp.reshape(1, columns),
        inject_nodes,
        node_diag.reshape(1, node_count),
        blocks,
        pattern,
        local_inv,
        iface_nodes,
        iface_count,
        iface_wt,
        aggregate.reshape(1, node_count),
        coarse_inv,
    )


def solution(mesh):
    in_specs = (
        P("groups", "sub"),
        P("groups"),
        P(None, "groups"),
        P("sub"),
        P("sub", None, None, None),
        P("sub", None),
        P("sub", None, None),
        P("sub", None, None),
        P("sub", None),
        P("sub", None, None),
        P("sub"),
        P("sub", None),
    )
    out_specs = (P("groups", "sub"), P("groups", "sub"))
    return jax.shard_map(shards, mesh=mesh, in_specs=in_specs, out_specs=out_specs, check_vma=False)
```

```python
import functools
import jax
import jax.numpy as jnp
from jax import lax
from jax.experimental import pallas as pl
from jax.experimental.pallas import tpu as pltpu
from jax.sharding import PartitionSpec as P

ITERS = 3
OFFSETS = (-2, -1, 1, 2)
EPSILON = 1e-06
HIGH = lax.Precision.HIGHEST
F32 = jnp.float32
BF16 = jnp.bfloat16
NT = (((1,), (1,)), ((), ()))


def split(value):
    high = value.astype(BF16)
    low = (value - high.astype(F32)).astype(BF16)
    return jnp.concatenate([high, low], axis=0)


def nt_dot(left, right):
    return lax.dot_general(left, right, NT, preferred_element_type=F32)


def fold(product, columns, width):
    return (
        product[:columns, :width]
        + product[:columns, width:]
        + product[columns : 2 * columns, :width]
    )


def kernel(
    source_hbm,
    amp_ref,
    inject_ref,
    diag_ref,
    blocks_hbm,
    pattern_hbm,
    inverse_hbm,
    nodes_ref,
    count_ref,
    weight_ref,
    aggregate_ref,
    coarse_ref,
    x_hbm,
    u_hbm,
    r_hbm,
    w_hbm,
    step_ref,
    raw,
    raw_inv,
    mat,
    inv,
    onehot,
    split_v,
    split_l,
    member,
    extra,
    local,
    x_now,
    u_now,
    r_now,
    w_now,
    y_now,
    ap,
    scaled,
    tile,
    near_inv,
    sums,
    outbox,
    inbox,
    pattern_ref,
    load_sem,
    raw_sem,
    out_sem,
    sum_send,
    sum_recv,
    face_send,
    face_recv,
    near_send,
    near_recv,
):
    n_sub = lax.axis_size("sub")
    me = lax.axis_index("sub")
    columns, node_count = r_now.shape
    rows, kept, size, _ = blocks_hbm.shape
    agg = coarse_ref.shape[0]
    slots = nodes_ref.shape[2]
    double = 2 * columns
    near = [me + offset for offset in OFFSETS]
    there = [jnp.logical_and(other >= 0, other < n_sub) for other in near]

    def each(count, body, init=0):
        return lax.fori_loop(0, count, body, init, unroll=True)

    def others(body):
        def one(step, carry):
            body(lax.rem(me + step, n_sub))
            return carry

        lax.fori_loop(1, n_sub, one, 0, unroll=n_sub <= 16)

    def at(i):
        return pl.ds(pl.multiple_of(i * size, size), size)

    barrier = pltpu.get_barrier_semaphore()

    def greet(other):
        pl.semaphore_signal(
            barrier, inc=1, device_id={"sub": other}, device_id_type=pl.DeviceIdType.MESH
        )

    def block_copy(i):
        return pltpu.make_async_copy(blocks_hbm.at[i], raw.at[i], raw_sem.at[i])

    source_copy = pltpu.make_async_copy(source_hbm, r_now, load_sem.at[0])
    inverse_copy = pltpu.make_async_copy(inverse_hbm, raw_inv, load_sem.at[1])
    pattern_copy = pltpu.make_async_copy(pattern_hbm, pattern_ref, load_sem.at[2])
    source_copy.start()
    inverse_copy.start()
    pattern_copy.start()
    for i in range(rows):
        block_copy(i).start()
    others(greet)

    near_inv[0:agg, :] = coarse_ref[...]

    def blank(j):
        inbox[:, j] = jnp.zeros((ITERS,) + inbox.shape[2:], F32)
        near_inv[(1 + j) * agg : (2 + j) * agg, :] = jnp.zeros((agg, near_inv.shape[1]), F32)

    for j in range(4):
        pl.when(jnp.logical_not(there[j]))(functools.partial(blank, j))

    for j in range(4):
        live = lax.broadcasted_iota(jnp.int32, (1, slots), 1) < count_ref[0, j]
        scaled[:, j * slots : (j + 1) * slots] = jnp.where(
            live, weight_ref[0, j : j + 1, :], 0.0
        )
    span = 2 * size

    def build(c, carry):
        ids = lax.broadcasted_iota(jnp.int32, (span, slots), 0) + c * span
        for j in range(4):
            same = ids == nodes_ref[0, j : j + 1, :]
            onehot[
                pl.ds(pl.multiple_of(c * span, span), span), j * slots : (j + 1) * slots
            ] = jnp.where(same, 1.0, 0.0).astype(BF16)
        return carry

    lax.fori_loop(0, rows // 2, build, 0)

    tile[...] = jnp.zeros_like(tile)
    tile[0:2, 0:columns] = inject_ref[...].astype(F32)
    tile[2:3, 0:columns] = amp_ref[...]
    turned = tile[...].T
    first_node = me * node_count
    at_source = turned[:columns, 0:1].astype(jnp.int32) - first_node
    at_sink = turned[:columns, 1:2].astype(jnp.int32) - first_node
    amp = turned[:columns, 2:3]
    lane = lax.broadcasted_iota(jnp.int32, (columns, size), 1)
    agg_id = lax.broadcasted_iota(jnp.int32, (2 * agg, size), 0)
    source_copy.wait()
    for i in range(rows):
        place = slice(i * size, (i + 1) * size)
        node = lane + i * size
        hits = (node == at_source).astype(F32) - (node == at_sink).astype(F32)
        rhs = r_now[:, place] + amp * hits
        r_now[:, place] = rhs
        split_v[:, place] = split(rhs)
        belongs = (agg_id == aggregate_ref[:, place]).astype(F32).astype(BF16)
        member[:, place] = belongs
        split_l[i, double : double + 2 * agg, :] = belongs

    def sum_copy(stage, other):
        return pltpu.make_async_remote_copy(
            src_ref=sums.at[stage, me],
            dst_ref=sums.at[stage, me],
            send_sem=sum_send.at[stage],
            recv_sem=sum_recv.at[stage],
            device_id={"sub": other},
            device_id_type=pl.DeviceIdType.MESH,
        )

    def send_sums(stage):
        others(lambda other: sum_copy(stage, other).start())

    def all_sums(stage, sem):
        part = sums.at[stage, pl.ds(0, n_sub - 1)]
        return pltpu.make_async_copy(part, part, sem.at[stage])

    def face_copy(stage, j):
        depth = columns + agg if stage == 0 else columns
        return pltpu.make_async_remote_copy(
            src_ref=outbox.at[stage, j, pl.ds(0, depth)],
            dst_ref=inbox.at[stage, 3 - j, pl.ds(0, depth)],
            send_sem=face_send.at[stage, j],
            recv_sem=face_recv.at[stage, 3 - j],
            device_id={"sub": near[j]},
            device_id_type=pl.DeviceIdType.MESH,
        )

    def face_arrival(stage, j):
        depth = columns + agg if stage == 0 else columns
        part = inbox.at[stage, j, pl.ds(0, depth)]
        return pltpu.make_async_copy(part, part, face_recv.at[stage, j])

    def near_copy(j):
        return pltpu.make_async_remote_copy(
            src_ref=coarse_ref,
            dst_ref=near_inv.at[pl.ds((4 - j) * agg, agg)],
            send_sem=near_send.at[j],
            recv_sem=near_recv.at[3 - j],
            device_id={"sub": near[j]},
            device_id_type=pl.DeviceIdType.MESH,
        )

    def near_arrival(j):
        part = near_inv.at[pl.ds((1 + j) * agg, agg)]
        return pltpu.make_async_copy(part, part, near_recv.at[j])

    def dots_tile(dots):
        turned = jnp.concatenate(dots, axis=0).T
        part = jnp.sum(turned.reshape(size // 4, 4, double), axis=0)
        return jnp.concatenate([part[:, :columns], part[:, columns:]], axis=0)

    def step_of(stage):
        total = jnp.sum(sums[stage], axis=0)[:, columns:]
        top = jnp.sum(total[0:4], axis=0, keepdims=True)
        bottom = jnp.sum(total[4:8], axis=0, keepdims=True)
        line = top / (bottom + EPSILON)
        line = jnp.concatenate([line, line], axis=1)
        return jnp.broadcast_to(line, (size, double)).T[:columns]

    zero = jnp.zeros((columns, size), F32)
    dots = None
    pl.semaphore_wait(barrier, n_sub - 1)

    for stage in range(ITERS):
        coarse = nt_dot(member[...], split_v[...])[:agg]
        beside = dots_tile(dots) if stage else jnp.zeros((agg, columns), F32)
        sums[stage, me] = jnp.concatenate(
            [coarse[:, :columns] + coarse[:, columns:], beside], axis=1
        )
        send_sums(stage)
        if stage == 0:
            for j in range(4):
                pl.when(there[j])(near_copy(j).start)
            inverse_copy.wait()

        def solve(i, carry):
            if stage == 0:
                inv[i] = split(raw_inv[i])
            value = fold(nt_dot(split_v[:, at(i)], inv[i]), columns, size)
            local[:, at(i)] = value
            split_l[i, 0:double, :] = split(value)
            return carry

        each(rows, solve)

        depth = double + 2 * agg if stage == 0 else double
        left = jnp.concatenate([split_l[i, 0:depth, :] for i in range(rows)], axis=1)
        for j in range(4):
            got = jnp.dot(
                left, onehot[:, j * slots : (j + 1) * slots], preferred_element_type=F32
            )
            outbox[stage, j, 0:columns, :] = got[:columns] + got[columns:double]
            if stage == 0:
                outbox[stage, j, columns : columns + agg, :] = got[double : double + agg]
            pl.when(there[j])(face_copy(stage, j).start)
        if stage == 0:
            pattern_copy.wait()

        def apply(i, carry):
            if stage == 0:
                block_copy(i).wait()
                for k in range(kept):
                    mat[i, :, k * size : (k + 1) * size] = split(raw[i, k])
            picked = jnp.concatenate(
                [split_l[pattern_ref[i, k], 0:depth, :] for k in range(kept)], axis=1
            )
            product = nt_dot(picked, mat[i])
            diag = diag_ref[:, at(i)]
            y_now[:, at(i)] = fold(product, columns, size) + diag * local[:, at(i)]
            if stage == 0:
                own = product[double : double + agg]
                mine = split_l[i, double : double + 2 * agg, :].astype(F32)[:agg]
                ap[i, 0:agg, :] = own[:, :size] + own[:, size:] + diag * mine
            return carry

        each(rows, apply)

        all_sums(stage, sum_recv).wait()
        for j in range(4):
            if stage == 0:
                pl.when(there[j])(near_arrival(j).wait)
            pl.when(there[j])(face_arrival(stage, j).wait)

        gathered = sums[stage].reshape(n_sub * agg, double)
        coarse = jnp.dot(near_inv[...], gathered, precision=HIGH, preferred_element_type=F32)
        gap = jnp.zeros((agg, double), F32)
        tail = jnp.zeros((size - 11 * agg, double), F32)
        coarse_split = split(jnp.concatenate([coarse, gap, coarse, tail], axis=0).T[:columns])
        if stage:
            step = step_of(stage)

        pieces = [
            split(inbox[stage, j, 0:columns, :] * scaled[:, j * slots : (j + 1) * slots])
            for j in range(4)
        ]
        left = jnp.concatenate(pieces, axis=1)
        if stage == 0:
            strips = []
            for j in range(4):
                strip = inbox[stage, j, columns : columns + agg, :]
                strip = strip * scaled[:, j * slots : (j + 1) * slots]
                cells = [jnp.zeros((agg, slots), F32)] * 4
                cells[j] = strip
                strips.append(jnp.concatenate(cells, axis=1))
            left = jnp.concatenate([left, split(jnp.concatenate(strips, axis=0))], axis=0)

        def finish(c, dots):
            chunk = onehot[pl.ds(pl.multiple_of(c * span, span), span), :]
            scattered = nt_dot(left, chunk)
            for part in range(2):
                i = 2 * c + part
                piece = scattered[:, part * size : (part + 1) * size]
                if stage == 0:
                    outer = piece[double : double + 4 * agg] + piece[double + 4 * agg :]
                    ap[i, agg : 5 * agg, :] = -outer
                    high = ap[i].astype(BF16).astype(F32)
                    low = ap[i] - high
                    pad = jnp.zeros((agg, size), F32)
                    end = jnp.zeros((size - 11 * agg, size), F32)
                    extra[i, :, 0:size] = jnp.concatenate([high, pad, low, end], axis=0).astype(BF16)
                    mine = split_l[i, double : double + 2 * agg, :].astype(F32)[:agg]
                    extra[i, :, size : 2 * size] = jnp.concatenate(
                        [mine, jnp.zeros((size - agg, size), F32)], axis=0
                    ).astype(BF16)
                product = jnp.dot(coarse_split, extra[i], preferred_element_type=F32)
                product = product[:columns] + product[columns:]
                image = y_now[:, at(i)] - (piece[:columns] + piece[columns:double])
                image = image + product[:, :size]
                update = local[:, at(i)] + product[:, size:]
                residual = r_now[:, at(i)]
                if stage:
                    old_u, old_w = u_now[:, at(i)], w_now[:, at(i)]
                    advance = step * old_u
                    x_now[:, at(i)] = advance if stage == 1 else x_now[:, at(i)] + advance
                    residual = residual - step * old_w
                    r_now[:, at(i)] = residual
                    update, image = old_u - step * update, old_w - step * image
                u_now[:, at(i)] = update
                w_now[:, at(i)] = image
                if stage < ITERS - 1:
                    split_v[:, at(i)] = split(image)
                dots = [dots[0] + residual * image, dots[1] + image * image]
            return dots

        dots = each(rows // 2, finish, [zero, zero])

    sums[ITERS, me] = jnp.concatenate([jnp.zeros((agg, columns), F32), dots_tile(dots)], axis=1)
    send_sums(ITERS)
    leaving = [
        pltpu.make_async_copy(held, out, out_sem.at[place])
        for place, (held, out) in enumerate(
            ((x_now, x_hbm), (u_now, u_hbm), (r_now, r_hbm), (w_now, w_hbm))
        )
    ]
    for copy in leaving:
        copy.start()
    for j in range(4):
        pl.when(there[j])(near_copy(j).wait_send)
        for stage in range(ITERS):
            pl.when(there[j])(face_copy(stage, j).wait_send)
    for stage in range(ITERS + 1):
        all_sums(stage, sum_send).wait()
    all_sums(ITERS, sum_recv).wait()
    step_ref[...] = step_of(ITERS)
    for copy in leaving:
        copy.wait()


def shards(
    source_field,
    inject_amp,
    inject_nodes,
    node_diag,
    blocks,
    pattern,
    local_inv,
    iface_nodes,
    iface_count,
    iface_wt,
    aggregate,
    coarse_inv,
):
    columns, node_count = source_field.shape
    rows, kept, size, _ = blocks.shape
    agg, n_coarse = coarse_inv.shape
    slots = iface_wt.shape[2]
    n_sub = lax.axis_size("sub")
    vmem = pl.BlockSpec(memory_space=pltpu.VMEM)
    smem = pl.BlockSpec(memory_space=pltpu.SMEM)
    far = pl.BlockSpec(memory_space=pl.ANY)
    field = jax.ShapeDtypeStruct((columns, node_count), F32)
    held = pltpu.VMEM((columns, node_count), F32)
    dma = pltpu.SemaphoreType.DMA
    x, u, r, w, step = pl.pallas_call(
        kernel,
        out_shape=(field, field, field, field, jax.ShapeDtypeStruct((columns, size), F32)),
        in_specs=[far, vmem, vmem, vmem, far, far, far, vmem, smem, vmem, vmem, vmem],
        out_specs=(far, far, far, far, vmem),
        scratch_shapes=[
            pltpu.VMEM((rows, kept, size, size), F32),
            pltpu.VMEM((rows, size, size), F32),
            pltpu.VMEM((rows, 2 * size, kept * size), BF16),
            pltpu.VMEM((rows, 2 * size, size), BF16),
            pltpu.VMEM((node_count, 4 * slots), BF16),
            pltpu.VMEM((2 * columns, node_count), BF16),
            pltpu.VMEM((rows, 2 * columns + 2 * agg, size), BF16),
            pltpu.VMEM((2 * agg, node_count), BF16),
            pltpu.VMEM((rows, size, 2 * size), BF16),
            held,
            held,
            held,
            held,
            held,
            held,
            pltpu.VMEM((rows, 5 * agg, size), F32),
            pltpu.VMEM((1, 4 * slots), F32),
            pltpu.VMEM((size, size), F32),
            pltpu.VMEM((5 * agg, n_coarse), F32),
            pltpu.VMEM((ITERS + 1, n_sub, agg, 2 * columns), F32),
            pltpu.VMEM((ITERS, 4, columns + agg, slots), F32),
            pltpu.VMEM((ITERS, 4, columns + agg, slots), F32),
            pltpu.SMEM((rows, kept), jnp.int32),
            dma((3,)),
            dma((rows,)),
            dma((4,)),
            dma((ITERS + 1,)),
            dma((ITERS + 1,)),
            dma((ITERS, 4)),
            dma((ITERS, 4)),
            dma((4,)),
            dma((4,)),
        ],
        compiler_params=pltpu.CompilerParams(
            collective_id=0, has_side_effects=True, vmem_limit_bytes=56 * 1024 * 1024
        ),
        cost_estimate=pl.CostEstimate(
            flops=4_000_000_000, bytes_accessed=12_000_000, transcendentals=0
        ),
    )(
        source_field,
        inject_amp.reshape(1, columns),
        inject_nodes,
        node_diag.reshape(1, node_count),
        blocks,
        pattern,
        local_inv,
        iface_nodes,
        iface_count,
        iface_wt,
        aggregate.reshape(1, node_count),
        coarse_inv,
    )
    step = step[:, :1]
    return x + step * u, r - step * w


def solution(mesh):
    in_specs = (
        P("groups", "sub"),
        P("groups"),
        P(None, "groups"),
        P("sub"),
        P("sub", None, None, None),
        P("sub", None),
        P("sub", None, None),
        P("sub", None, None),
        P("sub", None),
        P("sub", None, None),
        P("sub"),
        P("sub", None),
    )
    out_specs = (P("groups", "sub"), P("groups", "sub"))
    return jax.shard_map(shards, mesh=mesh, in_specs=in_specs, out_specs=out_specs, check_vma=False)
```

```python
import functools
import jax
import jax.numpy as jnp
from jax import lax
from jax.experimental import pallas as pl
from jax.experimental.pallas import tpu as pltpu
from jax.sharding import PartitionSpec as P

ITERS = 3
OFFSETS = (-2, -1, 1, 2)
EPSILON = 1e-06
HIGH = lax.Precision.HIGHEST
F32 = jnp.float32
BF16 = jnp.bfloat16
NT = (((1,), (1,)), ((), ()))


def split(value):
    high = value.astype(BF16)
    low = (value - high.astype(F32)).astype(BF16)
    return jnp.concatenate([high, low], axis=0)


def nt_dot(left, right):
    return lax.dot_general(left, right, NT, preferred_element_type=F32)


def fold(product, columns, width):
    return (
        product[:columns, :width]
        + product[:columns, width:]
        + product[columns : 2 * columns, :width]
    )


def kernel(
    source_hbm,
    amp_ref,
    inject_ref,
    diag_ref,
    blocks_hbm,
    pattern_hbm,
    inverse_hbm,
    nodes_ref,
    count_ref,
    weight_ref,
    aggregate_ref,
    coarse_ref,
    x_now,
    r_now,
    raw,
    raw_inv,
    mat,
    inv,
    onehot,
    split_v,
    split_l,
    member,
    extra,
    local,
    u_now,
    w_now,
    y_now,
    ap,
    scaled,
    tile,
    near_inv,
    sums,
    outbox,
    inbox,
    pattern_ref,
    load_sem,
    raw_sem,
    sum_send,
    sum_recv,
    face_send,
    face_recv,
    near_send,
    near_recv,
):
    n_sub = lax.axis_size("sub")
    me = lax.axis_index("sub")
    columns, node_count = r_now.shape
    rows, kept, size, _ = blocks_hbm.shape
    agg = coarse_ref.shape[0]
    slots = nodes_ref.shape[2]
    double = 2 * columns
    near = [me + offset for offset in OFFSETS]
    there = [jnp.logical_and(other >= 0, other < n_sub) for other in near]

    def each(count, body, init=0):
        return lax.fori_loop(0, count, body, init, unroll=True)

    def others(body):
        def one(step, carry):
            body(lax.rem(me + step, n_sub))
            return carry

        lax.fori_loop(1, n_sub, one, 0, unroll=n_sub <= 16)

    def at(i):
        return pl.ds(pl.multiple_of(i * size, size), size)

    barrier = pltpu.get_barrier_semaphore()

    def greet(other):
        pl.semaphore_signal(
            barrier, inc=1, device_id={"sub": other}, device_id_type=pl.DeviceIdType.MESH
        )

    def block_copy(i):
        return pltpu.make_async_copy(blocks_hbm.at[i], raw.at[i], raw_sem.at[i])

    source_copy = pltpu.make_async_copy(source_hbm, r_now, load_sem.at[0])
    inverse_copy = pltpu.make_async_copy(inverse_hbm, raw_inv, load_sem.at[1])
    pattern_copy = pltpu.make_async_copy(pattern_hbm, pattern_ref, load_sem.at[2])
    source_copy.start()
    inverse_copy.start()
    pattern_copy.start()
    for i in range(rows):
        block_copy(i).start()
    others(greet)

    near_inv[0:agg, :] = coarse_ref[...]

    def blank(j):
        inbox[:, j] = jnp.zeros((ITERS,) + inbox.shape[2:], F32)
        near_inv[(1 + j) * agg : (2 + j) * agg, :] = jnp.zeros((agg, near_inv.shape[1]), F32)

    for j in range(4):
        pl.when(jnp.logical_not(there[j]))(functools.partial(blank, j))

    for j in range(4):
        live = lax.broadcasted_iota(jnp.int32, (1, slots), 1) < count_ref[0, j]
        scaled[:, j * slots : (j + 1) * slots] = jnp.where(
            live, weight_ref[0, j : j + 1, :], 0.0
        )
    span = 2 * size

    def build(c, carry):
        ids = lax.broadcasted_iota(jnp.int32, (span, slots), 0) + c * span
        for j in range(4):
            same = ids == nodes_ref[0, j : j + 1, :]
            onehot[
                pl.ds(pl.multiple_of(c * span, span), span), j * slots : (j + 1) * slots
            ] = jnp.where(same, 1.0, 0.0).astype(BF16)
        return carry

    lax.fori_loop(0, rows // 2, build, 0)

    tile[...] = jnp.zeros_like(tile)
    tile[0:2, 0:columns] = inject_ref[...].astype(F32)
    tile[2:3, 0:columns] = amp_ref[...]
    turned = tile[...].T
    first_node = me * node_count
    at_source = turned[:columns, 0:1].astype(jnp.int32) - first_node
    at_sink = turned[:columns, 1:2].astype(jnp.int32) - first_node
    amp = turned[:columns, 2:3]
    lane = lax.broadcasted_iota(jnp.int32, (columns, size), 1)
    agg_id = lax.broadcasted_iota(jnp.int32, (2 * agg, size), 0)
    source_copy.wait()
    for i in range(rows):
        place = slice(i * size, (i + 1) * size)
        node = lane + i * size
        hits = (node == at_source).astype(F32) - (node == at_sink).astype(F32)
        rhs = r_now[:, place] + amp * hits
        r_now[:, place] = rhs
        split_v[:, place] = split(rhs)
        belongs = (agg_id == aggregate_ref[:, place]).astype(F32).astype(BF16)
        member[:, place] = belongs
        split_l[i, double : double + 2 * agg, :] = belongs

    def sum_copy(stage, other):
        return pltpu.make_async_remote_copy(
            src_ref=sums.at[stage, me],
            dst_ref=sums.at[stage, me],
            send_sem=sum_send.at[stage],
            recv_sem=sum_recv.at[stage],
            device_id={"sub": other},
            device_id_type=pl.DeviceIdType.MESH,
        )

    def send_sums(stage):
        others(lambda other: sum_copy(stage, other).start())

    def all_sums(stage, sem):
        part = sums.at[stage, pl.ds(0, n_sub - 1)]
        return pltpu.make_async_copy(part, part, sem.at[stage])

    def face_copy(stage, j):
        depth = columns + agg if stage == 0 else columns
        return pltpu.make_async_remote_copy(
            src_ref=outbox.at[stage, j, pl.ds(0, depth)],
            dst_ref=inbox.at[stage, 3 - j, pl.ds(0, depth)],
            send_sem=face_send.at[stage, j],
            recv_sem=face_recv.at[stage, 3 - j],
            device_id={"sub": near[j]},
            device_id_type=pl.DeviceIdType.MESH,
        )

    def face_arrival(stage, j):
        depth = columns + agg if stage == 0 else columns
        part = inbox.at[stage, j, pl.ds(0, depth)]
        return pltpu.make_async_copy(part, part, face_recv.at[stage, j])

    def near_copy(j):
        return pltpu.make_async_remote_copy(
            src_ref=coarse_ref,
            dst_ref=near_inv.at[pl.ds((4 - j) * agg, agg)],
            send_sem=near_send.at[j],
            recv_sem=near_recv.at[3 - j],
            device_id={"sub": near[j]},
            device_id_type=pl.DeviceIdType.MESH,
        )

    def near_arrival(j):
        part = near_inv.at[pl.ds((1 + j) * agg, agg)]
        return pltpu.make_async_copy(part, part, near_recv.at[j])

    def dots_tile(dots):
        turned = jnp.concatenate(dots, axis=0).T
        part = jnp.sum(turned.reshape(size // 4, 4, double), axis=0)
        return jnp.concatenate([part[:, :columns], part[:, columns:]], axis=0)

    def step_of(stage):
        total = jnp.sum(sums[stage], axis=0)[:, columns:]
        top = jnp.sum(total[0:4], axis=0, keepdims=True)
        bottom = jnp.sum(total[4:8], axis=0, keepdims=True)
        line = top / (bottom + EPSILON)
        line = jnp.concatenate([line, line], axis=1)
        return jnp.broadcast_to(line, (size, double)).T[:columns]

    zero = jnp.zeros((columns, size), F32)
    dots = None
    pl.semaphore_wait(barrier, n_sub - 1)

    for stage in range(ITERS):
        coarse = nt_dot(member[...], split_v[...])[:agg]
        beside = dots_tile(dots) if stage else jnp.zeros((agg, columns), F32)
        sums[stage, me] = jnp.concatenate(
            [coarse[:, :columns] + coarse[:, columns:], beside], axis=1
        )
        send_sums(stage)
        if stage == 0:
            for j in range(4):
                pl.when(there[j])(near_copy(j).start)
            inverse_copy.wait()

        def solve(i, carry):
            if stage == 0:
                inv[i] = split(raw_inv[i])
            value = fold(nt_dot(split_v[:, at(i)], inv[i]), columns, size)
            local[:, at(i)] = value
            split_l[i, 0:double, :] = split(value)
            return carry

        each(rows, solve)

        depth = double + 2 * agg if stage == 0 else double
        left = jnp.concatenate([split_l[i, 0:depth, :] for i in range(rows)], axis=1)
        for j in range(4):
            got = jnp.dot(
                left, onehot[:, j * slots : (j + 1) * slots], preferred_element_type=F32
            )
            outbox[stage, j, 0:columns, :] = got[:columns] + got[columns:double]
            if stage == 0:
                outbox[stage, j, columns : columns + agg, :] = got[double : double + agg]
            pl.when(there[j])(face_copy(stage, j).start)
        if stage == 0:
            pattern_copy.wait()

        def apply(i, carry):
            if stage == 0:
                block_copy(i).wait()
                for k in range(kept):
                    mat[i, :, k * size : (k + 1) * size] = split(raw[i, k])
            picked = jnp.concatenate(
                [split_l[pattern_ref[k, i], 0:depth, :] for k in range(kept)], axis=1
            )
            product = nt_dot(picked, mat[i])
            diag = diag_ref[:, at(i)]
            y_now[:, at(i)] = fold(product, columns, size) + diag * local[:, at(i)]
            if stage == 0:
                own = product[double : double + agg]
                mine = split_l[i, double : double + 2 * agg, :].astype(F32)[:agg]
                ap[i, 0:agg, :] = own[:, :size] + own[:, size:] + diag * mine
            return carry

        each(rows, apply)

        all_sums(stage, sum_recv).wait()
        for j in range(4):
            if stage == 0:
                pl.when(there[j])(near_arrival(j).wait)
            pl.when(there[j])(face_arrival(stage, j).wait)

        gathered = sums[stage].reshape(n_sub * agg, double)
        coarse = jnp.dot(near_inv[...], gathered, precision=HIGH, preferred_element_type=F32)
        gap = jnp.zeros((agg, double), F32)
        tail = jnp.zeros((size - 11 * agg, double), F32)
        coarse_split = split(jnp.concatenate([coarse, gap, coarse, tail], axis=0).T[:columns])
        if stage:
            step = step_of(stage)

        pieces = [
            split(inbox[stage, j, 0:columns, :] * scaled[:, j * slots : (j + 1) * slots])
            for j in range(4)
        ]
        left = jnp.concatenate(pieces, axis=1)
        if stage == 0:
            strips = []
            for j in range(4):
                strip = inbox[stage, j, columns : columns + agg, :]
                strip = strip * scaled[:, j * slots : (j + 1) * slots]
                cells = [jnp.zeros((agg, slots), F32)] * 4
                cells[j] = strip
                strips.append(jnp.concatenate(cells, axis=1))
            left = jnp.concatenate([left, split(jnp.concatenate(strips, axis=0))], axis=0)

        def finish(c, dots):
            chunk = onehot[pl.ds(pl.multiple_of(c * span, span), span), :]
            scattered = nt_dot(left, chunk)
            for part in range(2):
                i = 2 * c + part
                piece = scattered[:, part * size : (part + 1) * size]
                if stage == 0:
                    outer = piece[double : double + 4 * agg] + piece[double + 4 * agg :]
                    ap[i, agg : 5 * agg, :] = -outer
                    high = ap[i].astype(BF16).astype(F32)
                    low = ap[i] - high
                    pad = jnp.zeros((agg, size), F32)
                    end = jnp.zeros((size - 11 * agg, size), F32)
                    extra[i, :, 0:size] = jnp.concatenate([high, pad, low, end], axis=0).astype(BF16)
                    mine = split_l[i, double : double + 2 * agg, :].astype(F32)[:agg]
                    extra[i, :, size : 2 * size] = jnp.concatenate(
                        [mine, jnp.zeros((size - agg, size), F32)], axis=0
                    ).astype(BF16)
                product = jnp.dot(coarse_split, extra[i], preferred_element_type=F32)
                product = product[:columns] + product[columns:]
                image = y_now[:, at(i)] - (piece[:columns] + piece[columns:double])
                image = image + product[:, :size]
                update = local[:, at(i)] + product[:, size:]
                residual = r_now[:, at(i)]
                if stage:
                    old_u, old_w = u_now[:, at(i)], w_now[:, at(i)]
                    advance = step * old_u
                    x_now[:, at(i)] = advance if stage == 1 else x_now[:, at(i)] + advance
                    residual = residual - step * old_w
                    r_now[:, at(i)] = residual
                    update, image = old_u - step * update, old_w - step * image
                u_now[:, at(i)] = update
                w_now[:, at(i)] = image
                if stage < ITERS - 1:
                    split_v[:, at(i)] = split(image)
                dots = [dots[0] + residual * image, dots[1] + image * image]
            return dots

        dots = each(rows // 2, finish, [zero, zero])

    sums[ITERS, me] = jnp.concatenate([jnp.zeros((agg, columns), F32), dots_tile(dots)], axis=1)
    send_sums(ITERS)
    for j in range(4):
        pl.when(there[j])(near_copy(j).wait_send)
        for stage in range(ITERS):
            pl.when(there[j])(face_copy(stage, j).wait_send)
    for stage in range(ITERS + 1):
        all_sums(stage, sum_send).wait()
    all_sums(ITERS, sum_recv).wait()
    step = step_of(ITERS)

    def close(i, carry):
        x_now[:, at(i)] = x_now[:, at(i)] + step * u_now[:, at(i)]
        r_now[:, at(i)] = r_now[:, at(i)] - step * w_now[:, at(i)]
        return carry

    each(rows, close)


def shards(
    source_field,
    inject_amp,
    inject_nodes,
    node_diag,
    blocks,
    pattern,
    local_inv,
    iface_nodes,
    iface_count,
    iface_wt,
    aggregate,
    coarse_inv,
):
    columns, node_count = source_field.shape
    rows, kept, size, _ = blocks.shape
    agg, n_coarse = coarse_inv.shape
    slots = iface_wt.shape[2]
    n_sub = lax.axis_size("sub")
    vmem = pl.BlockSpec(memory_space=pltpu.VMEM)
    smem = pl.BlockSpec(memory_space=pltpu.SMEM)
    far = pl.BlockSpec(memory_space=pl.ANY)
    held = pltpu.VMEM((columns, node_count), F32)
    dma = pltpu.SemaphoreType.DMA
    solution_out, residual_out = pl.pallas_call(
        kernel,
        out_shape=(held, held),
        in_specs=[far, vmem, vmem, vmem, far, far, far, vmem, smem, vmem, vmem, vmem],
        out_specs=(vmem, vmem),
        scratch_shapes=[
            pltpu.VMEM((rows, kept, size, size), F32),
            pltpu.VMEM((rows, size, size), F32),
            pltpu.VMEM((rows, 2 * size, kept * size), BF16),
            pltpu.VMEM((rows, 2 * size, size), BF16),
            pltpu.VMEM((node_count, 4 * slots), BF16),
            pltpu.VMEM((2 * columns, node_count), BF16),
            pltpu.VMEM((rows, 2 * columns + 2 * agg, size), BF16),
            pltpu.VMEM((2 * agg, node_count), BF16),
            pltpu.VMEM((rows, size, 2 * size), BF16),
            held,
            held,
            held,
            held,
            pltpu.VMEM((rows, 5 * agg, size), F32),
            pltpu.VMEM((1, 4 * slots), F32),
            pltpu.VMEM((size, size), F32),
            pltpu.VMEM((5 * agg, n_coarse), F32),
            pltpu.VMEM((ITERS + 1, n_sub, agg, 2 * columns), F32),
            pltpu.VMEM((ITERS, 4, columns + agg, slots), F32),
            pltpu.VMEM((ITERS, 4, columns + agg, slots), F32),
            pltpu.SMEM((kept, rows), jnp.int32),
            dma((3,)),
            dma((rows,)),
            dma((ITERS + 1,)),
            dma((ITERS + 1,)),
            dma((ITERS, 4)),
            dma((ITERS, 4)),
            dma((4,)),
            dma((4,)),
        ],
        compiler_params=pltpu.CompilerParams(
            collective_id=0, has_side_effects=True, vmem_limit_bytes=56 * 1024 * 1024
        ),
        cost_estimate=pl.CostEstimate(
            flops=4_000_000_000, bytes_accessed=12_000_000, transcendentals=0
        ),
    )(
        source_field,
        inject_amp.reshape(1, columns),
        inject_nodes,
        node_diag.reshape(1, node_count),
        blocks,
        pattern.T,
        local_inv,
        iface_nodes,
        iface_count,
        iface_wt,
        aggregate.reshape(1, node_count),
        coarse_inv,
    )
    return solution_out, residual_out


def solution(mesh):
    in_specs = (
        P("groups", "sub"),
        P("groups"),
        P(None, "groups"),
        P("sub"),
        P("sub", None, None, None),
        P("sub", None),
        P("sub", None, None),
        P("sub", None, None),
        P("sub", None),
        P("sub", None, None),
        P("sub"),
        P("sub", None),
    )
    out_specs = (P("groups", "sub"), P("groups", "sub"))
    return jax.shard_map(shards, mesh=mesh, in_specs=in_specs, out_specs=out_specs, check_vma=False)
```

```python
import functools
import jax
import jax.numpy as jnp
from jax import lax
from jax.experimental import pallas as pl
from jax.experimental.pallas import tpu as pltpu
from jax.sharding import PartitionSpec as P

ITERS = 3
OFFSETS = (-2, -1, 1, 2)
EPSILON = 1e-06
HIGH = lax.Precision.HIGHEST
F32 = jnp.float32
BF16 = jnp.bfloat16
NT = (((1,), (1,)), ((), ()))


def split(value):
    high = value.astype(BF16)
    low = (value - high.astype(F32)).astype(BF16)
    return jnp.concatenate([high, low], axis=0)


def nt_dot(left, right):
    return lax.dot_general(left, right, NT, preferred_element_type=F32)


def fold(product, columns, width):
    return (
        product[:columns, :width]
        + product[:columns, width:]
        + product[columns : 2 * columns, :width]
    )


def kernel(
    source_hbm,
    amp_ref,
    inject_ref,
    diag_ref,
    blocks_hbm,
    pattern_hbm,
    inverse_hbm,
    nodes_ref,
    count_ref,
    weight_ref,
    aggregate_ref,
    coarse_ref,
    x_now,
    r_now,
    raw,
    raw_inv,
    mat,
    inv,
    onehot,
    split_v,
    split_l,
    member,
    extra,
    local,
    u_now,
    w_now,
    y_now,
    ap,
    scaled,
    tile,
    near_inv,
    sums,
    outbox,
    inbox,
    pattern_ref,
    load_sem,
    raw_sem,
    sum_send,
    sum_recv,
    face_send,
    face_recv,
    near_send,
    near_recv,
):
    n_sub = lax.axis_size("sub")
    me = lax.axis_index("sub")
    columns, node_count = r_now.shape
    rows, kept, size, _ = blocks_hbm.shape
    agg = coarse_ref.shape[0]
    slots = nodes_ref.shape[2]
    double = 2 * columns
    near = [me + offset for offset in OFFSETS]
    there = [jnp.logical_and(other >= 0, other < n_sub) for other in near]

    def each(count, body, init=0):
        return lax.fori_loop(0, count, body, init, unroll=True)

    def others(body):
        def one(step, carry):
            body(lax.rem(me + step, n_sub))
            return carry

        lax.fori_loop(1, n_sub, one, 0, unroll=n_sub <= 16)

    def at(i):
        return pl.ds(pl.multiple_of(i * size, size), size)

    barrier = pltpu.get_barrier_semaphore()

    def greet(other):
        pl.semaphore_signal(
            barrier, inc=1, device_id={"sub": other}, device_id_type=pl.DeviceIdType.MESH
        )

    def block_copy(i):
        return pltpu.make_async_copy(blocks_hbm.at[i], raw.at[i], raw_sem.at[i])

    source_copy = pltpu.make_async_copy(source_hbm, r_now, load_sem.at[0])
    inverse_copy = pltpu.make_async_copy(inverse_hbm, raw_inv, load_sem.at[1])
    pattern_copy = pltpu.make_async_copy(pattern_hbm, pattern_ref, load_sem.at[2])
    others(greet)
    source_copy.start()
    inverse_copy.start()
    pattern_copy.start()
    for i in range(rows):
        block_copy(i).start()

    near_inv[0:agg, :] = coarse_ref[...]

    def blank(j):
        inbox[:, j] = jnp.zeros((ITERS,) + inbox.shape[2:], F32)
        near_inv[(1 + j) * agg : (2 + j) * agg, :] = jnp.zeros((agg, near_inv.shape[1]), F32)

    for j in range(4):
        pl.when(jnp.logical_not(there[j]))(functools.partial(blank, j))

    for j in range(4):
        live = lax.broadcasted_iota(jnp.int32, (1, slots), 1) < count_ref[0, j]
        scaled[:, j * slots : (j + 1) * slots] = jnp.where(
            live, weight_ref[0, j : j + 1, :], 0.0
        )
    span = 2 * size

    def build(c, carry):
        ids = lax.broadcasted_iota(jnp.int32, (span, slots), 0) + c * span
        for j in range(4):
            same = ids == nodes_ref[0, j : j + 1, :]
            onehot[
                pl.ds(pl.multiple_of(c * span, span), span), j * slots : (j + 1) * slots
            ] = jnp.where(same, 1.0, 0.0).astype(BF16)
        return carry

    lax.fori_loop(0, rows // 2, build, 0)

    tile[...] = jnp.zeros_like(tile)
    tile[0:2, 0:columns] = inject_ref[...].astype(F32)
    tile[2:3, 0:columns] = amp_ref[...]
    turned = tile[...].T
    first_node = me * node_count
    at_source = turned[:columns, 0:1].astype(jnp.int32) - first_node
    at_sink = turned[:columns, 1:2].astype(jnp.int32) - first_node
    amp = turned[:columns, 2:3]
    lane = lax.broadcasted_iota(jnp.int32, (columns, size), 1)
    agg_id = lax.broadcasted_iota(jnp.int32, (2 * agg, size), 0)
    source_copy.wait()
    for i in range(rows):
        place = slice(i * size, (i + 1) * size)
        node = lane + i * size
        hits = (node == at_source).astype(F32) - (node == at_sink).astype(F32)
        rhs = r_now[:, place] + amp * hits
        r_now[:, place] = rhs
        split_v[:, place] = split(rhs)
        belongs = (agg_id == aggregate_ref[:, place]).astype(F32).astype(BF16)
        member[:, place] = belongs
        split_l[i, double : double + 2 * agg, :] = belongs

    def sum_copy(stage, other):
        return pltpu.make_async_remote_copy(
            src_ref=sums.at[stage, me],
            dst_ref=sums.at[stage, me],
            send_sem=sum_send.at[stage],
            recv_sem=sum_recv.at[stage],
            device_id={"sub": other},
            device_id_type=pl.DeviceIdType.MESH,
        )

    def send_sums(stage):
        others(lambda other: sum_copy(stage, other).start())

    def all_sums(stage, sem):
        part = sums.at[stage, pl.ds(0, n_sub - 1)]
        return pltpu.make_async_copy(part, part, sem.at[stage])

    def face_copy(stage, j):
        depth = columns + agg if stage == 0 else columns
        return pltpu.make_async_remote_copy(
            src_ref=outbox.at[stage, j, pl.ds(0, depth)],
            dst_ref=inbox.at[stage, 3 - j, pl.ds(0, depth)],
            send_sem=face_send.at[stage, j],
            recv_sem=face_recv.at[stage, 3 - j],
            device_id={"sub": near[j]},
            device_id_type=pl.DeviceIdType.MESH,
        )

    def face_arrival(stage, j):
        depth = columns + agg if stage == 0 else columns
        part = inbox.at[stage, j, pl.ds(0, depth)]
        return pltpu.make_async_copy(part, part, face_recv.at[stage, j])

    def near_copy(j):
        return pltpu.make_async_remote_copy(
            src_ref=coarse_ref,
            dst_ref=near_inv.at[pl.ds((4 - j) * agg, agg)],
            send_sem=near_send.at[j],
            recv_sem=near_recv.at[3 - j],
            device_id={"sub": near[j]},
            device_id_type=pl.DeviceIdType.MESH,
        )

    def near_arrival(j):
        part = near_inv.at[pl.ds((1 + j) * agg, agg)]
        return pltpu.make_async_copy(part, part, near_recv.at[j])

    def dots_tile(dots):
        turned = jnp.concatenate(dots, axis=0).T
        part = jnp.sum(turned.reshape(size // 4, 4, double), axis=0)
        return jnp.concatenate([part[:, :columns], part[:, columns:]], axis=0)

    def step_of(stage):
        total = jnp.sum(sums[stage], axis=0)[:, columns:]
        top = jnp.sum(total[0:4], axis=0, keepdims=True)
        bottom = jnp.sum(total[4:8], axis=0, keepdims=True)
        line = top / (bottom + EPSILON)
        line = jnp.concatenate([line, line], axis=1)
        return jnp.broadcast_to(line, (size, double)).T[:columns]

    zero = jnp.zeros((columns, size), F32)
    dots = None

    for stage in range(ITERS):
        coarse = nt_dot(member[...], split_v[...])[:agg]
        beside = dots_tile(dots) if stage else jnp.zeros((agg, columns), F32)
        sums[stage, me] = jnp.concatenate(
            [coarse[:, :columns] + coarse[:, columns:], beside], axis=1
        )
        if stage:
            send_sums(stage)
        else:
            inverse_copy.wait()

        def solve(i, carry):
            if stage == 0:
                inv[i] = split(raw_inv[i])
            value = fold(nt_dot(split_v[:, at(i)], inv[i]), columns, size)
            local[:, at(i)] = value
            split_l[i, 0:double, :] = split(value)
            return carry

        each(rows, solve)
        if stage == 0:
            pl.semaphore_wait(barrier, n_sub - 1)
            send_sums(stage)
            for j in range(4):
                pl.when(there[j])(near_copy(j).start)

        depth = double + 2 * agg if stage == 0 else double
        left = jnp.concatenate([split_l[i, 0:depth, :] for i in range(rows)], axis=1)
        for j in range(4):
            got = jnp.dot(
                left, onehot[:, j * slots : (j + 1) * slots], preferred_element_type=F32
            )
            outbox[stage, j, 0:columns, :] = got[:columns] + got[columns:double]
            if stage == 0:
                outbox[stage, j, columns : columns + agg, :] = got[double : double + agg]
            pl.when(there[j])(face_copy(stage, j).start)
        if stage == 0:
            pattern_copy.wait()

        def apply(i, carry):
            if stage == 0:
                block_copy(i).wait()
                for k in range(kept):
                    mat[i, :, k * size : (k + 1) * size] = split(raw[i, k])
            picked = jnp.concatenate(
                [split_l[pattern_ref[k, i], 0:depth, :] for k in range(kept)], axis=1
            )
            product = nt_dot(picked, mat[i])
            diag = diag_ref[:, at(i)]
            y_now[:, at(i)] = fold(product, columns, size) + diag * local[:, at(i)]
            if stage == 0:
                own = product[double : double + agg]
                mine = split_l[i, double : double + 2 * agg, :].astype(F32)[:agg]
                ap[i, 0:agg, :] = own[:, :size] + own[:, size:] + diag * mine
            return carry

        each(rows, apply)

        all_sums(stage, sum_recv).wait()
        for j in range(4):
            if stage == 0:
                pl.when(there[j])(near_arrival(j).wait)
            pl.when(there[j])(face_arrival(stage, j).wait)

        gathered = sums[stage].reshape(n_sub * agg, double)
        coarse = jnp.dot(near_inv[...], gathered, precision=HIGH, preferred_element_type=F32)
        gap = jnp.zeros((agg, double), F32)
        tail = jnp.zeros((size - 11 * agg, double), F32)
        coarse_split = split(jnp.concatenate([coarse, gap, coarse, tail], axis=0).T[:columns])
        if stage:
            step = step_of(stage)

        pieces = [
            split(inbox[stage, j, 0:columns, :] * scaled[:, j * slots : (j + 1) * slots])
            for j in range(4)
        ]
        left = jnp.concatenate(pieces, axis=1)
        if stage == 0:
            strips = []
            for j in range(4):
                strip = inbox[stage, j, columns : columns + agg, :]
                strip = strip * scaled[:, j * slots : (j + 1) * slots]
                cells = [jnp.zeros((agg, slots), F32)] * 4
                cells[j] = strip
                strips.append(jnp.concatenate(cells, axis=1))
            left = jnp.concatenate([left, split(jnp.concatenate(strips, axis=0))], axis=0)

        def finish(c, dots):
            chunk = onehot[pl.ds(pl.multiple_of(c * span, span), span), :]
            scattered = nt_dot(left, chunk)
            for part in range(2):
                i = 2 * c + part
                piece = scattered[:, part * size : (part + 1) * size]
                if stage == 0:
                    outer = piece[double : double + 4 * agg] + piece[double + 4 * agg :]
                    ap[i, agg : 5 * agg, :] = -outer
                    high = ap[i].astype(BF16).astype(F32)
                    low = ap[i] - high
                    pad = jnp.zeros((agg, size), F32)
                    end = jnp.zeros((size - 11 * agg, size), F32)
                    extra[i, :, 0:size] = jnp.concatenate([high, pad, low, end], axis=0).astype(BF16)
                    mine = split_l[i, double : double + 2 * agg, :].astype(F32)[:agg]
                    extra[i, :, size : 2 * size] = jnp.concatenate(
                        [mine, jnp.zeros((size - agg, size), F32)], axis=0
                    ).astype(BF16)
                product = jnp.dot(coarse_split, extra[i], preferred_element_type=F32)
                product = product[:columns] + product[columns:]
                image = y_now[:, at(i)] - (piece[:columns] + piece[columns:double])
                image = image + product[:, :size]
                update = local[:, at(i)] + product[:, size:]
                residual = r_now[:, at(i)]
                if stage:
                    old_u, old_w = u_now[:, at(i)], w_now[:, at(i)]
                    advance = step * old_u
                    x_now[:, at(i)] = advance if stage == 1 else x_now[:, at(i)] + advance
                    residual = residual - step * old_w
                    r_now[:, at(i)] = residual
                    update, image = old_u - step * update, old_w - step * image
                u_now[:, at(i)] = update
                w_now[:, at(i)] = image
                if stage < ITERS - 1:
                    split_v[:, at(i)] = split(image)
                dots = [dots[0] + residual * image, dots[1] + image * image]
            return dots

        dots = each(rows // 2, finish, [zero, zero])

    sums[ITERS, me] = jnp.concatenate([jnp.zeros((agg, columns), F32), dots_tile(dots)], axis=1)
    send_sums(ITERS)
    for j in range(4):
        pl.when(there[j])(near_copy(j).wait_send)
        for stage in range(ITERS):
            pl.when(there[j])(face_copy(stage, j).wait_send)
    for stage in range(ITERS + 1):
        all_sums(stage, sum_send).wait()
    all_sums(ITERS, sum_recv).wait()
    step = step_of(ITERS)

    def close(i, carry):
        x_now[:, at(i)] = x_now[:, at(i)] + step * u_now[:, at(i)]
        r_now[:, at(i)] = r_now[:, at(i)] - step * w_now[:, at(i)]
        return carry

    each(rows, close)


def shards(
    source_field,
    inject_amp,
    inject_nodes,
    node_diag,
    blocks,
    pattern,
    local_inv,
    iface_nodes,
    iface_count,
    iface_wt,
    aggregate,
    coarse_inv,
):
    columns, node_count = source_field.shape
    rows, kept, size, _ = blocks.shape
    agg, n_coarse = coarse_inv.shape
    slots = iface_wt.shape[2]
    n_sub = lax.axis_size("sub")
    vmem = pl.BlockSpec(memory_space=pltpu.VMEM)
    smem = pl.BlockSpec(memory_space=pltpu.SMEM)
    far = pl.BlockSpec(memory_space=pl.ANY)
    held = pltpu.VMEM((columns, node_count), F32)
    dma = pltpu.SemaphoreType.DMA
    solution_out, residual_out = pl.pallas_call(
        kernel,
        out_shape=(held, held),
        in_specs=[far, vmem, vmem, vmem, far, far, far, vmem, smem, vmem, vmem, vmem],
        out_specs=(vmem, vmem),
        scratch_shapes=[
            pltpu.VMEM((rows, kept, size, size), F32),
            pltpu.VMEM((rows, size, size), F32),
            pltpu.VMEM((rows, 2 * size, kept * size), BF16),
            pltpu.VMEM((rows, 2 * size, size), BF16),
            pltpu.VMEM((node_count, 4 * slots), BF16),
            pltpu.VMEM((2 * columns, node_count), BF16),
            pltpu.VMEM((rows, 2 * columns + 2 * agg, size), BF16),
            pltpu.VMEM((2 * agg, node_count), BF16),
            pltpu.VMEM((rows, size, 2 * size), BF16),
            held,
            held,
            held,
            held,
            pltpu.VMEM((rows, 5 * agg, size), F32),
            pltpu.VMEM((1, 4 * slots), F32),
            pltpu.VMEM((size, size), F32),
            pltpu.VMEM((5 * agg, n_coarse), F32),
            pltpu.VMEM((ITERS + 1, n_sub, agg, 2 * columns), F32),
            pltpu.VMEM((ITERS, 4, columns + agg, slots), F32),
            pltpu.VMEM((ITERS, 4, columns + agg, slots), F32),
            pltpu.SMEM((kept, rows), jnp.int32),
            dma((3,)),
            dma((rows,)),
            dma((ITERS + 1,)),
            dma((ITERS + 1,)),
            dma((ITERS, 4)),
            dma((ITERS, 4)),
            dma((4,)),
            dma((4,)),
        ],
        compiler_params=pltpu.CompilerParams(
            collective_id=0, has_side_effects=True, vmem_limit_bytes=56 * 1024 * 1024
        ),
        cost_estimate=pl.CostEstimate(
            flops=4_000_000_000, bytes_accessed=12_000_000, transcendentals=0
        ),
    )(
        source_field,
        inject_amp.reshape(1, columns),
        inject_nodes,
        node_diag.reshape(1, node_count),
        blocks,
        pattern.T,
        local_inv,
        iface_nodes,
        iface_count,
        iface_wt,
        aggregate.reshape(1, node_count),
        coarse_inv,
    )
    return solution_out, residual_out


def solution(mesh):
    in_specs = (
        P("groups", "sub"),
        P("groups"),
        P(None, "groups"),
        P("sub"),
        P("sub", None, None, None),
        P("sub", None),
        P("sub", None, None),
        P("sub", None, None),
        P("sub", None),
        P("sub", None, None),
        P("sub"),
        P("sub", None),
    )
    out_specs = (P("groups", "sub"), P("groups", "sub"))
    return jax.shard_map(shards, mesh=mesh, in_specs=in_specs, out_specs=out_specs, check_vma=False)
```
